32 devices in a mesh: groups: 1, expert: 16 (over z, y, core), req: 2 (over x).
Axes of the slice: x: 2, y: 2, z: 4, core: 2. Of those that a mesh axis runs over, the one named last changes fastest.
Arguments:
- tree_hidden: bfloat16 [512, 3584], P(('groups', 'expert', 'req')), may hold values from -6 to 6
- expert_ids: int32 [512, 8], P(('groups', 'expert', 'req')), may hold values from 0 to 15, all different within a row; in each aligned block of 16 rows (0 to 15, 16 to 31, ...) at most 16 rows name the same one
- route_weights: float32 [512, 8], P(('groups', 'expert', 'req')), may hold values from 0.1 to 1
- w_up: bfloat16 [16, 3584, 1024], P('expert', None, 'req'), may hold values from -0.09375 to 0.09375
- w_down: bfloat16 [16, 1024, 3584], P('expert', None, 'req'), may hold values from -0.1875 to 0.1875
- accept_count: int32 [32], P(('groups', 'expert', 'req')), may hold values from 1 to 8
- accept_pos: int32 [32, 8], P(('groups', 'expert', 'req')), may hold values from 0 to 15, as said below
- draft_owner: int32 [32], P(('groups', 'expert', 'req')), may hold values from 0 to 1, as said below
- mtp_gain: float32 [3584], replicated, may hold values from 0.5 to 1.5
Outputs:
- layer_out: bfloat16 [512, 3584], P(('groups', 'expert', 'req'))
- draft_inputs: bfloat16 [32, 8, 3584], P(('groups', 'expert', 'req'))
The draws below stay inside these ranges and needn't reach their ends.
Inputs may be any that keep to these rules, and one draw needn't show every extreme that they name: `expert_ids`: in the rows of one device each expert is named by at most 16 rows. `accept_pos`: each row holds distinct tree positions in increasing order. `draft_owner`: the requests q with the same q // 2 have distinct owners.
All inputs are finite; a program needn't handle non-finite values.
Results may differ from the reference program's by a relative error of at most 0.0057.
Values may be sent and summed in bfloat16 or wider, within the bound.
No kernel may reach another device: no remote copies, remote signals or barrier semaphores. Data moves between devices by JAX's collectives and lax.ppermute only.
A program may use at most 64 MiB of HBM per device.

```python
import math
import jax
import jax.numpy as jnp
import numpy as np
from jax import lax

D = 3584
FF = 1024
TREE = 16
EXPERTS = 16
TOP = 8
CAP = 16
ACC = 8
REQUESTS = 32
TOKENS = 512
EXPERT_ROWS = 512
N_REQ = 2


def draw_accept_count(key, part):
    key = jax.random.fold_in(key, 11)
    counts = jax.random.randint(key, (REQUESTS,), 1, ACC + 1, dtype=jnp.int32)
    return counts.at[0].set(ACC)


def draw_accept_pos(key, part):
    key = jax.random.fold_in(key, 12)
    sub_keys = jax.random.split(key, REQUESTS)
    orders = jax.vmap(lambda single: jax.random.permutation(single, TREE))(sub_keys)
    return jnp.sort(orders[:, :ACC], axis=1).astype(jnp.int32)


def draw_draft_owner(key, part):
    key = jax.random.fold_in(key, 13)
    sub_keys = jax.random.split(key, REQUESTS // N_REQ)
    owners = jax.vmap(lambda single: jax.random.permutation(single, N_REQ))(sub_keys)
    return owners.reshape(-1).astype(jnp.int32)


def levels(rng, extent, cuts, least, high):
    gain = 1.0
    for axis_at, blocks in cuts:
        draws = jax.random.uniform(jax.random.fold_in(jax.random.fold_in(rng, 6), axis_at), (blocks,), jnp.float32, least / len(cuts), high / len(cuts))
        gain = gain * jnp.repeat(jnp.exp(draws), extent[axis_at] // blocks).reshape((-1,) + (1,) * (len(extent) - 1 - axis_at))
    return gain


def assign_block(rng, own, number, rows, number_of, top, most, skew):
    ranking = jax.random.permutation(rng, number_of)
    heavy_load, usual = load_shares(number_of, rows * top, most, skew, True), load_shares(number_of, rows * top, most, skew, False)
    places = jnp.arange(number_of)

    def named(tallies, rotation):
        used = int((tallies > 0).sum())
        fixed = max(1, used // 4)
        moved = fixed + (places - fixed + rotation * (used - fixed)) % max(1, number_of - fixed)
        return jnp.zeros((number_of,), jnp.int32).at[ranking[jnp.where(places < fixed, places, moved)]].set(jnp.asarray(tallies, jnp.int32))

    tallies = jnp.where(number % 4 == 0, named(heavy_load, number // 4), named(usual, number - number // 4 - 1))
    mixed = jax.random.permutation(jax.random.fold_in(own, 3), number_of)
    source_of, taker = mixed[0:number_of // 2 * 2:2], mixed[1:number_of // 2 * 2:2]
    room = jnp.minimum(tallies[source_of] - 1, most - tallies[taker]) // 2
    room = jnp.where((source_of == ranking[0]) | (taker == ranking[0]) | (tallies[taker] == 0), 0, jnp.maximum(room, 0))
    moved = jax.random.randint(jax.random.fold_in(own, 4), (number_of // 2,), 0, 1 << 20) % (room + 1)
    tallies = tallies.at[source_of].add(-moved).at[taker].add(moved)
    labels = jnp.searchsorted(jnp.cumsum(tallies), jnp.arange(rows * top), side="right").astype(jnp.int32)
    grid = labels.reshape(top, rows).T
    grid = grid[jax.random.permutation(jax.random.fold_in(own, 1), rows)]
    rotation = jax.random.randint(jax.random.fold_in(own, 2), (rows, 1), 0, top)
    return jnp.take_along_axis(grid, (jnp.arange(top)[None, :] + rotation) % top, axis=1)


def load_shares(count, total, reach, lean, full):
    weights = [(1 << 20) // math.isqrt(rank ** lean) + 1 for rank in range(1, count + 1)]
    largest = reach if full else min(reach, max(-(-total // count), total * weights[0] // sum(weights)))
    least = 1 if total - largest >= count - 1 else 0
    given, surplus = [largest] + [least] * (count - 1), total - largest - least * (count - 1)
    while surplus > 0:
        candidates = [i for i in range(1, count) if given[i] < largest] or [i for i in range(1, count) if given[i] < reach]
        whole, remaining = sum([weights[i] for i in candidates]), surplus
        for i in candidates:
            addition = min(reach - given[i], max(1, remaining * weights[i] // whole), surplus)
            given[i] = given[i] + addition
            surplus = surplus - addition
    return np.array(given)


def gaussian(stream_key, dims, scale, bound, pieces=(), kind=jnp.bfloat16):
    gain = levels(stream_key, dims, pieces, -0.22, 0.18) if pieces else 1.0
    array = jax.random.normal(stream_key, dims, jnp.float32) * scale * gain
    return jnp.minimum(jnp.maximum(array, -bound), bound).astype(kind)


def setup_inputs(seed: int = 0, part: int = 0) -> dict:
    splits = jax.random.split(jax.random.key(seed), 10)
    part_keys = jax.random.split(jax.random.fold_in(splits[9], part), 10)
    tree_hidden = gaussian(part_keys[0], (TOKENS, D), 1.0, 6.0, ((0, 32),))
    expert_ids_keys = jax.random.split(jax.random.fold_in(part_keys[1], 1), TOKENS // TREE)
    expert_ids_turns = jax.random.permutation(jax.random.fold_in(part_keys[1], 3), TOKENS // TREE)
    expert_ids = jax.vmap(lambda own, number: assign_block(jax.random.fold_in(part_keys[1], 2), own, number, TREE, EXPERTS, TOP, CAP, 2))(expert_ids_keys, expert_ids_turns).reshape((TOKENS, TOP))
    route_weights = jnp.clip(0.1 + 0.9 * jax.random.uniform(part_keys[2], (TOKENS, TOP), jnp.float32) ** levels(part_keys[2], (TOKENS, TOP), ((0, 32),), -0.2, 0.2), 0.1, 1.0)
    w_up = gaussian(splits[3], (EXPERTS, D, FF), D ** -0.5, 0.09375, ((0, 16), (2, 2)))
    w_down = gaussian(splits[4], (EXPERTS, FF, D), FF ** -0.5, 0.1875, ((0, 16), (2, 2)))
    accept_count = draw_accept_count(jax.random.fold_in(jax.random.fold_in(splits[9], part), 71), part)
    accept_pos = draw_accept_pos(jax.random.fold_in(jax.random.fold_in(splits[9], part), 71), part)
    draft_owner = draw_draft_owner(jax.random.fold_in(jax.random.fold_in(splits[9], part), 71), part)
    mtp_gain = jnp.clip(1.0 + 0.1 * jax.random.normal(splits[8], (D,), jnp.float32), 0.5, 1.5)
    return {"tree_hidden": tree_hidden, "expert_ids": expert_ids, "route_weights": route_weights, "w_up": w_up, "w_down": w_down, "accept_count": accept_count, "accept_pos": accept_pos, "draft_owner": draft_owner, "mtp_gain": mtp_gain}


def reference(tree_hidden, expert_ids, route_weights, w_up, w_down, accept_count, accept_pos, draft_owner, mtp_gain):

    def one_expert(total, inputs):
        expert, up_matrix, down_matrix = inputs
        matches = expert_ids == expert
        weight = lax.optimization_barrier(jnp.sum(jnp.where(matches, route_weights, jnp.zeros_like(route_weights)), axis=1))
        chosen = jnp.nonzero(jnp.any(matches, axis=1), size=EXPERT_ROWS, fill_value=TOKENS)[0].astype(jnp.int32)
        safe = jnp.minimum(chosen, TOKENS - 1).astype(jnp.int32)
        token_rows = tree_hidden[safe]
        hidden = jax.nn.silu(jnp.dot(token_rows, up_matrix, preferred_element_type=jnp.float32)).astype(jnp.bfloat16)
        produced = jnp.dot(hidden, down_matrix, preferred_element_type=jnp.float32).astype(jnp.bfloat16)
        scaled = weight[safe][:, None] * produced.astype(jnp.float32)
        return (total.at[chosen].add(scaled, mode='drop'), None)
    start_total = jnp.zeros((TOKENS, D), jnp.float32)
    experts_list = jnp.arange(EXPERTS, dtype=jnp.int32)
    total, _ = lax.scan(one_expert, start_total, (experts_list, w_up, w_down))
    layer_out = (tree_hidden.astype(jnp.float32) + total).astype(jnp.bfloat16)
    per_request = layer_out.reshape(REQUESTS, TREE, D)
    request_index = jnp.arange(REQUESTS, dtype=jnp.int32)
    picked = per_request[request_index[:, None], accept_pos]
    live = jnp.arange(ACC, dtype=jnp.int32)[None, :] < accept_count[:, None]
    picked = jnp.where(live[:, :, None], picked, jnp.zeros_like(picked))
    values = picked.astype(jnp.float32)
    scale = lax.rsqrt(lax.optimization_barrier(jnp.mean(values * values, axis=-1, keepdims=True)) + 1e-06)
    normed = (values * scale * mtp_gain[None, None, :]).astype(jnp.bfloat16)
    target = (request_index // N_REQ * N_REQ + draft_owner).astype(jnp.int32)
    draft_inputs = jnp.zeros_like(normed).at[target].set(normed)
    return (layer_out, draft_inputs)
```

```python
import jax
import jax.numpy as jnp
from jax import lax
from jax.sharding import PartitionSpec as P


def find_slots(route_ids, expert_count):
    flat_ids = route_ids.reshape(-1)
    matches = (flat_ids[:, None] == jnp.arange(expert_count, dtype=jnp.int32)[None, :]).astype(
        jnp.int32
    )
    earlier = jnp.cumsum(matches, axis=0) - matches
    return jnp.sum(earlier * matches, axis=1).reshape(route_ids.shape)


def send_matrix(target, length):
    places = jnp.arange(length, dtype=jnp.int32)
    return jnp.any(places[:, None, None] == target[None, :, :], axis=2).astype(jnp.bfloat16)


def capacity_of(tree_len, top_k, expert_count):
    return min(tree_len, max(4, 2 * tree_len * top_k // expert_count))


def routed_plan(
    tree_hidden,
    expert_ids,
    route_weights,
    w_up,
    w_down,
    accept_count,
    accept_pos,
    draft_owner,
    mtp_gain,
):
    expert_count = lax.axis_size("expert")
    req_count = lax.axis_size("req")
    tree_len, top_k = expert_ids.shape
    capacity = capacity_of(tree_len, top_k, expert_count)
    up_local = w_up[0]
    down_local = w_down[0]
    own_target = expert_ids * capacity + find_slots(expert_ids, expert_count)
    mapping = send_matrix(own_target, expert_count * capacity)
    outgoing = jnp.dot(mapping, tree_hidden, preferred_element_type=jnp.float32).astype(
        jnp.bfloat16
    )
    outgoing = outgoing.reshape(expert_count, capacity, -1)
    arrived = lax.all_to_all(outgoing, "expert", split_axis=0, concat_axis=0, tiled=True)
    activated = jax.nn.silu(
        jnp.dot(
            lax.all_gather(arrived.reshape(expert_count * capacity, -1), "req", axis=0, tiled=True),
            up_local,
            preferred_element_type=jnp.float32,
        )
    ).astype(jnp.bfloat16)
    produced = jnp.dot(
        lax.all_gather(activated, "req", axis=1, tiled=True),
        down_local,
        preferred_element_type=jnp.float32,
    ).astype(jnp.bfloat16)
    shaped = produced.reshape(req_count, expert_count, capacity, -1)
    returned = lax.all_to_all(
        lax.all_to_all(shaped, "expert", split_axis=1, concat_axis=1, tiled=True),
        "req",
        split_axis=0,
        concat_axis=3,
        tiled=True,
    )
    returned = returned.reshape(expert_count * capacity, -1)
    places = jnp.arange(expert_count * capacity, dtype=jnp.int32)
    combine = jnp.sum(
        jnp.where(own_target[:, :, None] == places[None, None, :], route_weights[:, :, None], 0.0),
        axis=1,
    )
    mixed = jnp.dot(combine, returned.astype(jnp.float32), precision=lax.Precision.HIGHEST)
    layer_local = (tree_hidden.astype(jnp.float32) + mixed).astype(jnp.bfloat16)
    selector = selector_of(accept_pos, accept_count, tree_len)
    accepted = jnp.dot(selector, layer_local, preferred_element_type=jnp.float32).astype(
        jnp.bfloat16
    )
    owner_mask = (jnp.arange(req_count, dtype=jnp.int32) == draft_owner[0])[:, None, None]
    parcel = jnp.where(owner_mask, accepted[None], jnp.zeros_like(accepted)[None])
    delivered = lax.all_to_all(parcel, "req", split_axis=0, concat_axis=0, tiled=True)
    incoming = jnp.sum(delivered.astype(jnp.float32), axis=0)
    return (layer_local, norm_rows(incoming, mtp_gain))


def selector_of(accept_pos, accept_count, tree_len):
    accept_len = accept_pos.shape[1]
    position_hit = accept_pos[0][:, None] == jnp.arange(tree_len, dtype=jnp.int32)[None, :]
    live = jnp.arange(accept_len, dtype=jnp.int32)[:, None] < accept_count[0]
    return (position_hit & live).astype(jnp.bfloat16)


def norm_rows(rows, gain):
    scale = lax.rsqrt(jnp.mean(rows * rows, axis=-1, keepdims=True) + 1e-06)
    return (rows * scale * gain[None, :]).astype(jnp.bfloat16)[None]


def swap(array, axis, bit):
    size = lax.axis_size(axis)
    return lax.ppermute(array, axis, [(i, i ^ bit) for i in range(size)])


def three_parts(value):
    first = value.astype(jnp.bfloat16)
    rest = value - first.astype(jnp.float32)
    second = rest.astype(jnp.bfloat16)
    third = (rest - second.astype(jnp.float32)).astype(jnp.bfloat16)
    return [first, second, third]


CORE, Y, NEAR, FAR = ("expert", 1), ("expert", 2), ("expert", 4), ("expert", 8)
X = ("req", 1)


def gather(block, steps):
    for axis, bit in steps:
        block = jnp.concatenate([block, swap(block, axis, bit)], axis=0)
    return block


def gathered_plan(
    tree_hidden,
    expert_ids,
    route_weights,
    w_up,
    w_down,
    accept_count,
    accept_pos,
    draft_owner,
    mtp_gain,
):
    expert_count = lax.axis_size("expert")
    tree_len, features = tree_hidden.shape
    accept_len = accept_pos.shape[1]
    me = lax.axis_index("expert")
    side = lax.axis_index("req")
    hidden_half = w_up.shape[2]
    feature_half = w_down.shape[2]
    half = tree_len // 2

    w_own = lax.dynamic_slice_in_dim(w_down[0], side * hidden_half, hidden_half, 0)
    w_other = lax.dynamic_slice_in_dim(w_down[0], (1 - side) * hidden_half, hidden_half, 0)

    experts = jnp.arange(expert_count, dtype=jnp.int32)
    dense = jnp.sum(
        jnp.where(expert_ids[:, :, None] == experts[None, None, :], route_weights[:, :, None], 0.0),
        axis=1,
    )
    selector = selector_of(accept_pos, accept_count, tree_len)
    selector = jnp.pad(selector, ((0, tree_len - accept_len), (0, 0)))
    extra = jnp.concatenate(three_parts(dense) + [selector], axis=1)
    extra = jnp.pad(extra, ((0, 0), (0, -extra.shape[1] % 128)))
    rows = jnp.concatenate([tree_hidden, extra], axis=1)

    steps = [(FAR, NEAR, Y, X, CORE), (FAR, NEAR, X, Y, CORE)]
    blocks = [gather(rows[k * half : (k + 1) * half], steps[k]) for k in range(2)]

    here = (experts == me).astype(jnp.float32)
    own, weight = [], []
    for k in range(2):
        own.append(
            jax.nn.silu(
                jnp.dot(blocks[k][:, :features], w_up[0], preferred_element_type=jnp.float32)
            ).astype(jnp.bfloat16)
        )
        parts = blocks[k][:, features:].astype(jnp.float32)
        total = sum(parts[:, j * expert_count : (j + 1) * expert_count] for j in range(3))
        weight.append(jnp.sum(total * here[None, :], axis=1, keepdims=True))
    other = []
    for k in range(2):
        below = 1 << steps[k].index(X)
        turned = own[k].reshape(-1, 2, below * half, hidden_half)[:, ::-1]
        other.append(swap(turned.reshape(own[k].shape), *X))
    sums = []
    for k in range(2):
        produced = jnp.dot(own[k], w_own, preferred_element_type=jnp.float32) + jnp.dot(
            other[k], w_other, preferred_element_type=jnp.float32
        )
        sums.append(produced.astype(jnp.bfloat16).astype(jnp.float32) * weight[k])

    back = [(CORE, Y, NEAR, FAR), (CORE, NEAR, Y, FAR)]
    done = []
    for k in range(2):
        names = list(reversed(steps[k]))
        total = sums[k].reshape((2,) * len(names) + (half, feature_half))
        for step in back[k]:
            at = names.index(step)
            keep = lax.index_in_dim(total, 0, at, keepdims=False)
            send = lax.index_in_dim(total, 1, at, keepdims=False).astype(jnp.bfloat16)
            shape = keep.shape
            received = swap(send.reshape(-1, feature_half), *step).reshape(shape)
            total = keep + received.astype(jnp.float32)
            names.remove(step)
        done.append(total)
    mixed = jnp.concatenate(done, axis=1)

    place = [len(set(steps[k][: steps[k].index(X)])) for k in range(2)]
    second = jnp.concatenate(
        [blocks[k][half << place[k] : (half << place[k]) + half] for k in range(2)], axis=0
    )
    pair_hidden = jnp.stack([tree_hidden, second[:, :features]])
    pair_part = lax.dynamic_slice_in_dim(pair_hidden, side * feature_half, feature_half, 2)
    layer_part = (pair_part.astype(jnp.float32) + mixed).astype(jnp.bfloat16)
    received = swap(layer_part.reshape(2 * tree_len, feature_half), *X)
    received = received.reshape(2, tree_len, feature_half)[::-1]
    layer_pair = jnp.where(
        side == 0,
        jnp.concatenate([layer_part, received], axis=2),
        jnp.concatenate([received, layer_part], axis=2),
    )
    layer_local = layer_pair[0]
    at = features + 3 * expert_count
    stays = draft_owner[0] == side
    chosen = jnp.where(stays, layer_local, layer_pair[1])
    chosen_selector = jnp.where(stays, rows[:accept_len, at : at + tree_len], second[:accept_len, at : at + tree_len])
    incoming = jnp.dot(chosen_selector, chosen, preferred_element_type=jnp.float32)
    return (layer_local, norm_rows(incoming, mtp_gain))


def solution(mesh):
    def local(*arrays):
        tree_len, top_k = arrays[1].shape
        expert_count = mesh.shape["expert"]
        whole = capacity_of(tree_len, top_k, expert_count) == tree_len
        if whole and expert_count == 16 and mesh.shape["req"] == 2:
            return gathered_plan(*arrays)
        return routed_plan(*arrays)

    return jax.shard_map(
        local,
        mesh=mesh,
        in_specs=(
            P(("groups", "expert", "req"), None),
            P(("groups", "expert", "req"), None),
            P(("groups", "expert", "req"), None),
            P("expert", None, "req"),
            P("expert", None, "req"),
            P(("groups", "expert", "req")),
            P(("groups", "expert", "req"), None),
            P(("groups", "expert", "req")),
            P(),
        ),
        out_specs=(
            P(("groups", "expert", "req"), None),
            P(("groups", "expert", "req"), None, None),
        ),
        check_vma=False,
    )
```

```python
import jax
import jax.numpy as jnp
from jax import lax
from jax.sharding import PartitionSpec as P


def find_slots(route_ids, expert_count):
    flat_ids = route_ids.reshape(-1)
    matches = (flat_ids[:, None] == jnp.arange(expert_count, dtype=jnp.int32)[None, :]).astype(
        jnp.int32
    )
    earlier = jnp.cumsum(matches, axis=0) - matches
    return jnp.sum(earlier * matches, axis=1).reshape(route_ids.shape)


def send_matrix(target, length):
    places = jnp.arange(length, dtype=jnp.int32)
    return jnp.any(places[:, None, None] == target[None, :, :], axis=2).astype(jnp.bfloat16)


def capacity_of(tree_len, top_k, expert_count):
    return min(tree_len, max(4, 2 * tree_len * top_k // expert_count))


def routed_plan(
    tree_hidden,
    expert_ids,
    route_weights,
    w_up,
    w_down,
    accept_count,
    accept_pos,
    draft_owner,
    mtp_gain,
):
    expert_count = lax.axis_size("expert")
    req_count = lax.axis_size("req")
    tree_len, top_k = expert_ids.shape
    capacity = capacity_of(tree_len, top_k, expert_count)
    up_local = w_up[0]
    down_local = w_down[0]
    own_target = expert_ids * capacity + find_slots(expert_ids, expert_count)
    mapping = send_matrix(own_target, expert_count * capacity)
    outgoing = jnp.dot(mapping, tree_hidden, preferred_element_type=jnp.float32).astype(
        jnp.bfloat16
    )
    outgoing = outgoing.reshape(expert_count, capacity, -1)
    arrived = lax.all_to_all(outgoing, "expert", split_axis=0, concat_axis=0, tiled=True)
    activated = jax.nn.silu(
        jnp.dot(
            lax.all_gather(arrived.reshape(expert_count * capacity, -1), "req", axis=0, tiled=True),
            up_local,
            preferred_element_type=jnp.float32,
        )
    ).astype(jnp.bfloat16)
    produced = jnp.dot(
        lax.all_gather(activated, "req", axis=1, tiled=True),
        down_local,
        preferred_element_type=jnp.float32,
    ).astype(jnp.bfloat16)
    shaped = produced.reshape(req_count, expert_count, capacity, -1)
    returned = lax.all_to_all(
        lax.all_to_all(shaped, "expert", split_axis=1, concat_axis=1, tiled=True),
        "req",
        split_axis=0,
        concat_axis=3,
        tiled=True,
    )
    returned = returned.reshape(expert_count * capacity, -1)
    places = jnp.arange(expert_count * capacity, dtype=jnp.int32)
    combine = jnp.sum(
        jnp.where(own_target[:, :, None] == places[None, None, :], route_weights[:, :, None], 0.0),
        axis=1,
    )
    mixed = jnp.dot(combine, returned.astype(jnp.float32), precision=lax.Precision.HIGHEST)
    layer_local = (tree_hidden.astype(jnp.float32) + mixed).astype(jnp.bfloat16)
    selector = selector_of(accept_pos, accept_count, tree_len)
    accepted = jnp.dot(selector, layer_local, preferred_element_type=jnp.float32).astype(
        jnp.bfloat16
    )
    owner_mask = (jnp.arange(req_count, dtype=jnp.int32) == draft_owner[0])[:, None, None]
    parcel = jnp.where(owner_mask, accepted[None], jnp.zeros_like(accepted)[None])
    delivered = lax.all_to_all(parcel, "req", split_axis=0, concat_axis=0, tiled=True)
    incoming = jnp.sum(delivered.astype(jnp.float32), axis=0)
    return (layer_local, norm_rows(incoming, mtp_gain))


def selector_of(accept_pos, accept_count, tree_len):
    accept_len = accept_pos.shape[1]
    position_hit = accept_pos[0][:, None] == jnp.arange(tree_len, dtype=jnp.int32)[None, :]
    live = jnp.arange(accept_len, dtype=jnp.int32)[:, None] < accept_count[0]
    return (position_hit & live).astype(jnp.bfloat16)


def norm_rows(rows, gain):
    scale = lax.rsqrt(jnp.mean(rows * rows, axis=-1, keepdims=True) + 1e-06)
    return (rows * scale * gain[None, :]).astype(jnp.bfloat16)[None]


X, CORE, Y, NEAR, FAR = 1, 2, 4, 8, 16


def swap(array, name, bit, bit_on_second_core=None):
    bits = (bit, bit if bit_on_second_core is None else bit_on_second_core)
    size = lax.axis_size("expert") * lax.axis_size("req")
    pairs = [(i, i ^ bits[1 if i & CORE else 0]) for i in range(size)]
    with jax.named_scope(name):
        return lax.ppermute(array, ("expert", "req"), pairs)


def three_parts(value):
    first = value.astype(jnp.bfloat16)
    rest = value - first.astype(jnp.float32)
    second = rest.astype(jnp.bfloat16)
    third = (rest - second.astype(jnp.float32)).astype(jnp.bfloat16)
    return [first, second, third]


def blocks_of(array, order, length):
    return jnp.concatenate([array[i * length : (i + 1) * length] for i in order], axis=0)


def gathered_plan(
    tree_hidden,
    expert_ids,
    route_weights,
    w_up,
    w_down,
    accept_count,
    accept_pos,
    draft_owner,
    mtp_gain,
):
    expert_count = lax.axis_size("expert")
    tree_len, features = tree_hidden.shape
    accept_len = accept_pos.shape[1]
    me = lax.axis_index("expert")
    first_core = me % 2 == 0
    side = lax.axis_index("req")
    hidden_half = w_up.shape[2]
    feature_half = w_down.shape[2]

    half = tree_len // 2

    experts = jnp.arange(expert_count, dtype=jnp.int32)
    dense = jnp.sum(
        jnp.where(expert_ids[:, :, None] == experts[None, None, :], route_weights[:, :, None], 0.0),
        axis=1,
    )
    selector = selector_of(accept_pos, accept_count, tree_len)
    selector = jnp.pad(selector, ((0, tree_len - accept_len), (0, 0)))
    extra = jnp.concatenate(three_parts(dense) + [selector], axis=1)
    width = extra.shape[1]
    extra = jnp.concatenate([extra[:half], extra[half:]], axis=1)
    extra = jnp.pad(extra, ((0, 0), (0, -extra.shape[1] % 128)))

    there = swap(tree_hidden, "rows", FAR, NEAR)
    extra_there = swap(extra, "extra", FAR, NEAR)
    blocks = [
        jnp.concatenate([tree_hidden[:half], there[:half]], axis=0),
        jnp.concatenate(
            [
                jnp.concatenate([tree_hidden[half:], there[half:]], axis=0),
                jnp.concatenate([extra, extra_there], axis=0),
            ],
            axis=1,
        ),
    ]
    for step, bits in ((1, (NEAR, FAR)), (2, (Y, X)), (3, (X, Y))):
        blocks = [
            jnp.concatenate([blocks[k], swap(blocks[k], f"rows_{k}_{step}", *bits)], axis=0)
            for k in range(2)
        ]
    own = blocks
    other = [swap(own[k], f"rows_{k}_core", CORE) for k in range(2)]

    here = (experts == me).astype(jnp.float32)

    def up(part):
        return jax.nn.silu(
            jnp.dot(part[:, :features], w_up[0], preferred_element_type=jnp.float32)
        ).astype(jnp.bfloat16)

    def weights(block, chunk):
        at = features + chunk * width
        parts = block[:, at : at + 3 * expert_count].astype(jnp.float32)
        total = sum(parts[:, j * expert_count : (j + 1) * expert_count] for j in range(3))
        return jnp.sum(total * here[None, :], axis=1, keepdims=True)

    w_late = lax.optimization_barrier((w_down[0], own[0][:1, :128]))[0]
    w_own = lax.dynamic_slice_in_dim(w_late, side * hidden_half, hidden_half, 0)
    w_other = lax.dynamic_slice_in_dim(w_late, (1 - side) * hidden_half, hidden_half, 0)

    span = own[0].shape[0]
    last = lambda part: blocks_of(part, (1, 0), span // 2)
    last_but_one = lambda part: blocks_of(part, (1, 0, 3, 2), span // 4)

    order_first = [x * 8 + near * 2 + far for x in (0, 1) for near in (0, 1) for far in (0, 1)]
    order_second = [y * 8 + x * 4 + far * 2 for x in (0, 1) for y in (0, 1) for far in (0, 1)]

    acts, acts_there = [], []
    for k in range(2):
        acts.append((up(own[k]), up(other[k])))
        turned = (
            jnp.where(first_core, last(acts[k][0]), last_but_one(acts[k][0])),
            jnp.where(first_core, last_but_one(acts[k][1]), last(acts[k][1])),
        )
        acts_there.append(swap(jnp.concatenate(turned, axis=0), f"acts_{k}", X))

    sums = []
    for k in range(2):

        def down(acts_here, acts_there, block):
            produced = jnp.dot(acts_here, w_own, preferred_element_type=jnp.float32) + jnp.dot(
                acts_there, w_other, preferred_element_type=jnp.float32
            )
            return produced.astype(jnp.bfloat16).astype(jnp.float32) * weights(block, k)

        away = down(acts[k][1], acts_there[k][span:], other[1]).astype(jnp.bfloat16)
        total = down(acts[k][0], acts_there[k][:span], own[1])
        total = total + swap(away, f"sums_{k}_core", CORE).astype(jnp.float32)
        away = jnp.where(
            first_core,
            blocks_of(total, [i + 4 for i in order_first], half),
            blocks_of(total, [i + 1 for i in order_second], half),
        ).astype(jnp.bfloat16)
        total = jnp.where(
            first_core, blocks_of(total, order_first, half), blocks_of(total, order_second, half)
        )
        total = total + swap(away, f"sums_{k}_0", Y, NEAR).astype(jnp.float32)
        for step, bits in ((1, (NEAR, Y)), (2, (FAR, FAR))):
            shaped = total.reshape(2, 2, -1, feature_half)
            away = shaped[:, 1].reshape(-1, feature_half).astype(jnp.bfloat16)
            received = swap(away, f"sums_{k}_{step}", *bits)
            total = shaped[:, 0].reshape(-1, feature_half) + received.astype(jnp.float32)
        sums.append(total.reshape(2, half, feature_half))
    total = jnp.concatenate(sums, axis=1).reshape(2 * tree_len, feature_half)

    second = [
        jnp.where(first_core, block[8 * half : 9 * half], block[4 * half : 5 * half])
        for block in own
    ]
    pair_hidden = jnp.concatenate([tree_hidden, second[0], second[1][:, :features]], axis=0)
    pair_part = lax.dynamic_slice_in_dim(pair_hidden, side * feature_half, feature_half, 1)
    layer_part = (pair_part.astype(jnp.float32) + total).astype(jnp.bfloat16)
    received = blocks_of(swap(layer_part, "layer", X), (1, 0), tree_len)
    layer_pair = jnp.where(
        side == 0,
        jnp.concatenate([layer_part, received], axis=1),
        jnp.concatenate([received, layer_part], axis=1),
    )
    layer_local = layer_pair[:tree_len]
    stays = draft_owner[0] == side
    chosen = jnp.where(stays, layer_local, layer_pair[tree_len:])
    at = features + 3 * expert_count
    there = jnp.concatenate([second[1][:, at : at + tree_len], second[1][:, at + width : at + width + tree_len]], axis=0)
    chosen_selector = jnp.where(stays, selector, there)[:accept_len]
    incoming = jnp.dot(chosen_selector, chosen, preferred_element_type=jnp.float32)
    return (layer_local, norm_rows(incoming, mtp_gain))


def solution(mesh):
    def local(*arrays):
        tree_len, top_k = arrays[1].shape
        expert_count = mesh.shape["expert"]
        whole = capacity_of(tree_len, top_k, expert_count) == tree_len
        if whole and expert_count == 16 and mesh.shape["req"] == 2:
            return gathered_plan(*arrays)
        return routed_plan(*arrays)

    return jax.shard_map(
        local,
        mesh=mesh,
        in_specs=(
            P(("groups", "expert", "req"), None),
            P(("groups", "expert", "req"), None),
            P(("groups", "expert", "req"), None),
            P("expert", None, "req"),
            P("expert", None, "req"),
            P(("groups", "expert", "req")),
            P(("groups", "expert", "req"), None),
            P(("groups", "expert", "req")),
            P(),
        ),
        out_specs=(
            P(("groups", "expert", "req"), None),
            P(("groups", "expert", "req"), None, None),
        ),
        check_vma=False,
    )
```

```python
import jax
import jax.numpy as jnp
from jax import lax
from jax.experimental import pallas as pl
from jax.experimental.pallas import tpu as pltpu
from jax.sharding import PartitionSpec as P


def find_slots(route_ids, expert_count):
    flat_ids = route_ids.reshape(-1)
    matches = (flat_ids[:, None] == jnp.arange(expert_count, dtype=jnp.int32)[None, :]).astype(
        jnp.int32
    )
    earlier = jnp.cumsum(matches, axis=0) - matches
    return jnp.sum(earlier * matches, axis=1).reshape(route_ids.shape)


def send_matrix(target, length):
    places = jnp.arange(length, dtype=jnp.int32)
    return jnp.any(places[:, None, None] == target[None, :, :], axis=2).astype(jnp.bfloat16)


def capacity_of(tree_len, top_k, expert_count):
    return min(tree_len, max(4, 2 * tree_len * top_k // expert_count))


def routed_plan(
    tree_hidden,
    expert_ids,
    route_weights,
    w_up,
    w_down,
    accept_count,
    accept_pos,
    draft_owner,
    mtp_gain,
):
    expert_count = lax.axis_size("expert")
    req_count = lax.axis_size("req")
    tree_len, top_k = expert_ids.shape
    capacity = capacity_of(tree_len, top_k, expert_count)
    up_local = w_up[0]
    down_local = w_down[0]
    own_target = expert_ids * capacity + find_slots(expert_ids, expert_count)
    mapping = send_matrix(own_target, expert_count * capacity)
    outgoing = jnp.dot(mapping, tree_hidden, preferred_element_type=jnp.float32).astype(
        jnp.bfloat16
    )
    outgoing = outgoing.reshape(expert_count, capacity, -1)
    arrived = lax.all_to_all(outgoing, "expert", split_axis=0, concat_axis=0, tiled=True)
    activated = jax.nn.silu(
        jnp.dot(
            lax.all_gather(arrived.reshape(expert_count * capacity, -1), "req", axis=0, tiled=True),
            up_local,
            preferred_element_type=jnp.float32,
        )
    ).astype(jnp.bfloat16)
    produced = jnp.dot(
        lax.all_gather(activated, "req", axis=1, tiled=True),
        down_local,
        preferred_element_type=jnp.float32,
    ).astype(jnp.bfloat16)
    shaped = produced.reshape(req_count, expert_count, capacity, -1)
    returned = lax.all_to_all(
        lax.all_to_all(shaped, "expert", split_axis=1, concat_axis=1, tiled=True),
        "req",
        split_axis=0,
        concat_axis=3,
        tiled=True,
    )
    returned = returned.reshape(expert_count * capacity, -1)
    places = jnp.arange(expert_count * capacity, dtype=jnp.int32)
    combine = jnp.sum(
        jnp.where(own_target[:, :, None] == places[None, None, :], route_weights[:, :, None], 0.0),
        axis=1,
    )
    mixed = jnp.dot(combine, returned.astype(jnp.float32), precision=lax.Precision.HIGHEST)
    layer_local = (tree_hidden.astype(jnp.float32) + mixed).astype(jnp.bfloat16)
    selector = selector_of(accept_pos, accept_count, tree_len)
    accepted = jnp.dot(selector, layer_local, preferred_element_type=jnp.float32).astype(
        jnp.bfloat16
    )
    owner_mask = (jnp.arange(req_count, dtype=jnp.int32) == draft_owner[0])[:, None, None]
    parcel = jnp.where(owner_mask, accepted[None], jnp.zeros_like(accepted)[None])
    delivered = lax.all_to_all(parcel, "req", split_axis=0, concat_axis=0, tiled=True)
    incoming = jnp.sum(delivered.astype(jnp.float32), axis=0)
    return (layer_local, norm_rows(incoming, mtp_gain))


def selector_of(accept_pos, accept_count, tree_len):
    accept_len = accept_pos.shape[1]
    position_hit = accept_pos[0][:, None] == jnp.arange(tree_len, dtype=jnp.int32)[None, :]
    live = jnp.arange(accept_len, dtype=jnp.int32)[:, None] < accept_count[0]
    return (position_hit & live).astype(jnp.bfloat16)


def norm_rows(rows, gain):
    scale = lax.rsqrt(jnp.mean(rows * rows, axis=-1, keepdims=True) + 1e-06)
    return (rows * scale * gain[None, :]).astype(jnp.bfloat16)[None]


X, CORE, Y, NEAR, FAR = 1, 2, 4, 8, 16


def swap(array, name, bit, bit_on_second_core=None):
    bits = (bit, bit if bit_on_second_core is None else bit_on_second_core)
    size = lax.axis_size("expert") * lax.axis_size("req")
    pairs = [(i, i ^ bits[1 if i & CORE else 0]) for i in range(size)]
    with jax.named_scope(name):
        return lax.ppermute(array, ("expert", "req"), pairs)


def beside_kernel(count_ref, pos_ref, ids_ref, route_ref, out_ref):
    top_k, tree_len = ids_ref.shape
    half, wide = tree_len // 2, out_ref.shape[1]
    expert = lax.broadcasted_iota(jnp.int32, (tree_len, tree_len), 0)
    dense = jnp.zeros((tree_len, tree_len), jnp.float32)
    for k in range(top_k):
        dense = jnp.where(expert == ids_ref[k : k + 1], route_ref[k : k + 1], dense)
    row = lax.broadcasted_iota(jnp.int32, (tree_len, wide), 0)
    column = lax.broadcasted_iota(jnp.int32, (tree_len, wide), 1)
    sides = [jnp.zeros((tree_len, wide), jnp.float32) for _ in range(2)]
    for part in range(3):
        rounded = dense.astype(jnp.bfloat16)
        dense = dense - rounded.astype(jnp.float32)
        for k in range(2):
            spread = column == row + (part * tree_len + k * wide // 2)
            sides[k] += lax.dot_general(
                rounded,
                spread.astype(jnp.bfloat16),
                (((0,), (0,)), ((), ())),
                preferred_element_type=jnp.float32,
            )
    both = sides[0][:half] + sides[1][half:]
    for a in range(pos_ref.shape[1]):
        at = (a // half) * (wide // 2) + 3 * tree_len + pos_ref[0, a]
        hit = (row[:half] == a % half) & (column[:half] == at) & (a < count_ref[0])
        both = jnp.where(hit, 1.0, both)
    out_ref[...] = both.astype(jnp.bfloat16)


def beside(expert_ids, route_weights, accept_count, accept_pos):
    vmem, smem = pl.BlockSpec(memory_space=pltpu.VMEM), pl.BlockSpec(memory_space=pltpu.SMEM)
    return pl.pallas_call(
        beside_kernel,
        out_shape=jax.ShapeDtypeStruct((expert_ids.shape[0] // 2, 128), jnp.bfloat16),
        in_specs=[smem, smem, vmem, vmem],
        out_specs=vmem,
        name="beside_rows",
    )(accept_count, accept_pos, expert_ids.T, route_weights.T)


def blocks_of(array, order, length):
    return jnp.concatenate([array[i * length : (i + 1) * length] for i in order], axis=0)


def gathered_plan(
    tree_hidden,
    expert_ids,
    route_weights,
    w_up,
    w_down,
    accept_count,
    accept_pos,
    draft_owner,
    mtp_gain,
):
    expert_count = lax.axis_size("expert")
    tree_len, features = tree_hidden.shape
    accept_len = accept_pos.shape[1]
    me = lax.axis_index("expert")
    first_core = me % 2 == 0
    side = lax.axis_index("req")
    hidden_half = w_up.shape[2]
    feature_half = w_down.shape[2]

    half = tree_len // 2

    experts = jnp.arange(expert_count, dtype=jnp.int32)
    width = 64

    there = swap(tree_hidden, "rows", FAR, NEAR)
    extra = beside(expert_ids, route_weights, accept_count, accept_pos)
    extra_there = swap(extra, "extra", FAR, NEAR)
    blocks = [
        jnp.concatenate([tree_hidden[:half], there[:half]], axis=0),
        jnp.concatenate(
            [
                jnp.concatenate([tree_hidden[half:], there[half:]], axis=0),
                jnp.concatenate([extra, extra_there], axis=0),
            ],
            axis=1,
        ),
    ]
    for step, bits in ((1, (NEAR, FAR)), (2, (Y, X)), (3, (X, Y))):
        blocks = [
            jnp.concatenate([blocks[k], swap(blocks[k], f"rows_{k}_{step}", *bits)], axis=0)
            for k in range(2)
        ]
    own = blocks
    other = [swap(own[k], f"rows_{k}_core", CORE) for k in range(2)]

    here = (experts == me).astype(jnp.float32)

    def up(part):
        return jax.nn.silu(
            jnp.dot(part[:, :features], w_up[0], preferred_element_type=jnp.float32)
        ).astype(jnp.bfloat16)

    def weights(block, chunk):
        at = features + chunk * width
        parts = block[:, at : at + 3 * expert_count].astype(jnp.float32)
        total = sum(parts[:, j * expert_count : (j + 1) * expert_count] for j in range(3))
        return jnp.sum(total * here[None, :], axis=1, keepdims=True)

    w_late = lax.optimization_barrier((w_down[0], own[0][:1, :128]))[0]
    w_own = lax.dynamic_slice_in_dim(w_late, side * hidden_half, hidden_half, 0)
    w_other = lax.dynamic_slice_in_dim(w_late, (1 - side) * hidden_half, hidden_half, 0)

    span = own[0].shape[0]
    last = lambda part: blocks_of(part, (1, 0), span // 2)
    last_but_one = lambda part: blocks_of(part, (1, 0, 3, 2), span // 4)

    order_first = [x * 8 + near * 2 + far for x in (0, 1) for near in (0, 1) for far in (0, 1)]
    order_second = [y * 8 + x * 4 + far * 2 for x in (0, 1) for y in (0, 1) for far in (0, 1)]

    acts, acts_there = [], []
    for k in range(2):
        both = up(jnp.concatenate([own[k][:, :features], other[k][:, :features]], axis=0))
        acts.append((both[:span], both[span:]))
        turned = (
            jnp.where(first_core, last(acts[k][0]), last_but_one(acts[k][0])),
            jnp.where(first_core, last_but_one(acts[k][1]), last(acts[k][1])),
        )
        acts_there.append(swap(jnp.concatenate(turned, axis=0), f"acts_{k}", X))

    sums = []
    for k in range(2):

        def down(acts_here, acts_there, block):
            produced = jnp.dot(acts_here, w_own, preferred_element_type=jnp.float32) + jnp.dot(
                acts_there, w_other, preferred_element_type=jnp.float32
            )
            return produced.astype(jnp.bfloat16).astype(jnp.float32) * weights(block, k)

        away = down(acts[k][1], acts_there[k][span:], other[1]).astype(jnp.bfloat16)
        total = down(acts[k][0], acts_there[k][:span], own[1])
        total = total + swap(away, f"sums_{k}_core", CORE).astype(jnp.float32)
        away = jnp.where(
            first_core,
            blocks_of(total, [i + 4 for i in order_first], half),
            blocks_of(total, [i + 1 for i in order_second], half),
        ).astype(jnp.bfloat16)
        total = jnp.where(
            first_core, blocks_of(total, order_first, half), blocks_of(total, order_second, half)
        )
        total = total + swap(away, f"sums_{k}_0", Y, NEAR).astype(jnp.float32)
        for step, bits in ((1, (NEAR, Y)), (2, (FAR, FAR))):
            shaped = total.reshape(2, 2, -1, feature_half)
            away = shaped[:, 1].reshape(-1, feature_half).astype(jnp.bfloat16)
            received = swap(away, f"sums_{k}_{step}", *bits)
            total = shaped[:, 0].reshape(-1, feature_half) + received.astype(jnp.float32)
        sums.append(total.reshape(2, half, feature_half))
    total = jnp.concatenate(sums, axis=1).reshape(2 * tree_len, feature_half)

    second = [
        jnp.where(first_core, block[8 * half : 9 * half], block[4 * half : 5 * half])
        for block in own
    ]
    pair_hidden = jnp.concatenate([tree_hidden, second[0], second[1][:, :features]], axis=0)
    pair_part = lax.dynamic_slice_in_dim(pair_hidden, side * feature_half, feature_half, 1)
    layer_part = (pair_part.astype(jnp.float32) + total).astype(jnp.bfloat16)
    received = blocks_of(swap(layer_part, "layer", X), (1, 0), tree_len)
    layer_pair = jnp.where(
        side == 0,
        jnp.concatenate([layer_part, received], axis=1),
        jnp.concatenate([received, layer_part], axis=1),
    )
    layer_local = layer_pair[:tree_len]
    stays = draft_owner[0] == side
    chosen = jnp.where(stays, layer_local, layer_pair[tree_len:])
    at = features + 3 * expert_count
    own_beside = extra[:, at - features : at - features + tree_len]
    there_beside = second[1][:, at : at + tree_len]
    chosen_selector = jnp.where(stays, own_beside, there_beside)[:accept_len]
    incoming = jnp.dot(chosen_selector, chosen, preferred_element_type=jnp.float32)
    return (layer_local, norm_rows(incoming, mtp_gain))


def solution(mesh):
    def local(*arrays):
        tree_len, top_k = arrays[1].shape
        expert_count = mesh.shape["expert"]
        whole = capacity_of(tree_len, top_k, expert_count) == tree_len
        if whole and tree_len == expert_count == 16 and mesh.shape["req"] == 2:
            return gathered_plan(*arrays)
        return routed_plan(*arrays)

    return jax.shard_map(
        local,
        mesh=mesh,
        in_specs=(
            P(("groups", "expert", "req"), None),
            P(("groups", "expert", "req"), None),
            P(("groups", "expert", "req"), None),
            P("expert", None, "req"),
            P("expert", None, "req"),
            P(("groups", "expert", "req")),
            P(("groups", "expert", "req"), None),
            P(("groups", "expert", "req")),
            P(),
        ),
        out_specs=(
            P(("groups", "expert", "req"), None),
            P(("groups", "expert", "req"), None, None),
        ),
        check_vma=False,
    )
```
